512 devices in a mesh: dp: 8 (over z), expert: 64 (over x, y, core).
Axes of the slice: x: 4, y: 8, z: 8, core: 2. Of those that a mesh axis runs over, the one named last changes fastest.
Arguments:
- tokens: bfloat16 [65536, 1024], P(('dp', 'expert')), may hold values from -6 to 6
- cotangent: bfloat16 [65536, 1024], P(('dp', 'expert')), may hold values from -6 to 6
- routes: int32 [65536, 8], P(('dp', 'expert')), may hold values from 0 to 63, as said below
- combine: float32 [65536, 8], P(('dp', 'expert')), may hold values from 0.1 to 0.5
- w_gate: bfloat16 [64, 1024, 384], P('expert', 'dp'), may hold values from -0.1875 to 0.1875
- w_up: bfloat16 [64, 1024, 384], P('expert', 'dp'), may hold values from -0.1875 to 0.1875
- w_down: bfloat16 [64, 384, 1024], P('expert', None, 'dp'), may hold values from -0.3125 to 0.3125
Outputs:
- mixed: bfloat16 [65536, 1024], P(('dp', 'expert'))
- input_grad: bfloat16 [65536, 1024], P(('dp', 'expert'))
- combine_grad: float32 [65536, 8], P(('dp', 'expert'))
The draws below stay inside these ranges and needn't reach their ends.
Inputs may be any that keep to these rules, and one draw needn't show every extreme that they name: `routes`: each row names 8 different experts. Among the rows of one device (aligned blocks of 128 rows) each of 2 frequent experts, the same ones on every device, is named by 48 to 56 rows, and every other expert by at most 15 rows, with the counts of the other experts on one device differing by at most one. In every draw some device has a frequent expert named by exactly 56 rows and some device an other expert named by exactly 15 rows.
All inputs are finite; a program needn't handle non-finite values.
Results may differ from the reference program's by a relative error of at most 0.017.
Values may be sent and summed in bfloat16 or wider, within the bound.
No kernel may reach another device: no remote copies, remote signals or barrier semaphores. Data moves between devices by JAX's collectives and lax.ppermute only.
A program may use at most 128 MiB of HBM per device.

```python
import jax
import jax.numpy as jnp
from jax import lax

D = 1024
F = 384
TOPK = 8
HOT = 2
TOK_DEV = 128
EXPERTS = 64
HOT_MOST = 56
HOT_LEAST = 48
TOKENS = 65536


def draw_routes(key, part):
    base = jax.random.fold_in(key, 11)
    keys = jax.random.split(base, 8)
    blocks = TOKENS // TOK_DEV
    cold_count = EXPERTS - HOT
    order = jax.random.permutation(keys[0], EXPERTS).astype(jnp.int32)
    hot_ids = order[:HOT]
    cold_ids = order[HOT:]
    loads = jax.random.randint(keys[1], (blocks, HOT), HOT_LEAST, HOT_MOST + 1).astype(jnp.int32)
    busy = jax.random.randint(keys[2], (), 0, blocks).astype(jnp.int32)
    light = (busy + 1 + jax.random.randint(keys[3], (), 0, blocks - 1).astype(jnp.int32)) % blocks
    device_ids = jnp.arange(blocks, dtype=jnp.int32)
    loads = jnp.where((device_ids == busy)[:, None], HOT_MOST, loads)
    loads = jnp.where((device_ids == light)[:, None], HOT_LEAST, loads)
    place_keys = jax.random.split(keys[4], blocks * HOT)
    places = jax.vmap(lambda k: jax.random.permutation(k, TOK_DEV))(place_keys).reshape(blocks, HOT, TOK_DEV).astype(jnp.int32)
    picked = places < loads[:, :, None]
    picked_int = picked.astype(jnp.int32)
    hot_in_row = jnp.sum(picked_int, axis=1)
    hot_before = jnp.cumsum(picked_int, axis=1) - picked_int
    cold_need = TOPK - hot_in_row
    cold_start = jnp.cumsum(cold_need, axis=1) - cold_need
    offsets = jax.random.randint(keys[5], (blocks,), 0, cold_count).astype(jnp.int32)
    cold_keys = jax.random.split(keys[6], blocks)
    cold_order = jax.vmap(lambda k: jax.random.permutation(k, cold_count))(cold_keys).astype(jnp.int32)
    slot = jnp.arange(TOPK, dtype=jnp.int32)
    hot_match = picked[:, :, :, None] & (hot_before[:, :, :, None] == slot[None, None, None, :])
    hot_entry = jnp.sum(jnp.where(hot_match, hot_ids[None, :, None, None] + 1, 0), axis=1)
    cold_pos = (cold_start[:, :, None] + slot[None, None, :] - hot_in_row[:, :, None] + offsets[:, None, None]) % cold_count
    cold_pick = jnp.take_along_axis(cold_order, cold_pos.reshape(blocks, TOK_DEV * TOPK), axis=1).reshape(blocks, TOK_DEV, TOPK)
    cold_entry = cold_ids[cold_pick]
    chosen = jnp.where(slot[None, None, :] < hot_in_row[:, :, None], hot_entry - 1, cold_entry)
    column_keys = jax.random.split(keys[7], blocks * TOK_DEV)
    columns = jax.vmap(lambda k: jax.random.permutation(k, TOPK))(column_keys).astype(jnp.int32)
    routes = jnp.take_along_axis(chosen.reshape(blocks * TOK_DEV, TOPK), columns, axis=1)
    return routes.astype(jnp.int32)


def shard_levels(rng, extent, cuts, least, high):
    level, own = 1.0, jax.random.fold_in(rng, 6)
    for dim, parts in cuts:
        draws = jnp.exp(jax.random.uniform(jax.random.fold_in(own, dim), (parts,), jnp.float32, least / len(cuts), high / len(cuts)))
        level = level * jnp.repeat(draws, extent[dim] // parts).reshape([-1 if axis == dim else 1 for axis in range(len(extent))])
    return level


def normal_values(own_key, extent, deviation, limit, shards=(), held_as=jnp.bfloat16):
    values = deviation * jax.random.normal(own_key, extent, jnp.float32)
    if shards:
        values = values * shard_levels(own_key, extent, shards, -0.22, 0.18)
    return jnp.clip(values, -limit, limit).astype(held_as)


def setup_inputs(seed: int = 0) -> dict:
    streams_of = jax.random.split(jax.random.key(seed), 8)
    tokens = normal_values(streams_of[0], (TOKENS, D), 1.0, 6.0, ((0, 512),))
    cotangent = normal_values(streams_of[1], (TOKENS, D), 1.0, 6.0, ((0, 512),))
    routes = draw_routes(jax.random.fold_in(streams_of[7], 71), 0)
    combine = jnp.clip(0.1 + 0.4 * jax.random.uniform(streams_of[3], (TOKENS, TOPK), jnp.float32) ** shard_levels(streams_of[3], (TOKENS, TOPK), ((0, 512),), -0.2, 0.2), 0.1, 0.5)
    w_gate = normal_values(streams_of[4], (EXPERTS, D, F), D ** -0.5, 0.1875, ((0, 64), (1, 8)))
    w_up = normal_values(streams_of[5], (EXPERTS, D, F), D ** -0.5, 0.1875, ((0, 64), (1, 8)))
    w_down = normal_values(streams_of[6], (EXPERTS, F, D), F ** -0.5, 0.3125, ((0, 64), (2, 8)))
    return {"tokens": tokens, "cotangent": cotangent, "routes": routes, "combine": combine, "w_gate": w_gate, "w_up": w_up, "w_down": w_down}


def expert_rows(row_x, row_dy, row_g, wg, wu, wd):
    gate_pre = jnp.dot(row_x, wg, preferred_element_type=jnp.float32)
    up_proj = jnp.dot(row_x, wu, preferred_element_type=jnp.float32)
    sig = jax.nn.sigmoid(gate_pre)
    silu_val = gate_pre * sig
    hidden = (silu_val * up_proj).astype(jnp.bfloat16)
    expert_out = jnp.dot(hidden, wd, preferred_element_type=jnp.float32).astype(jnp.bfloat16)
    hidden_grad = row_g[:, None] * jnp.dot(row_dy, wd.T, preferred_element_type=jnp.float32)
    gate_grad = (hidden_grad * up_proj * sig * (1.0 + gate_pre * (1.0 - sig))).astype(jnp.bfloat16)
    up_grad = (hidden_grad * silu_val).astype(jnp.bfloat16)
    row_grad = jnp.dot(gate_grad, wg.T, preferred_element_type=jnp.float32) + jnp.dot(up_grad, wu.T, preferred_element_type=jnp.float32)
    return expert_out.astype(jnp.float32), row_grad.astype(jnp.bfloat16).astype(jnp.float32)


def reference(tokens, cotangent, routes, combine, w_gate, w_up, w_down):
    tok_rows, width = tokens.shape
    topk = routes.shape[1]
    pairs = tok_rows * topk
    flat_ids = routes.reshape(-1).astype(jnp.int32)
    order = jnp.argsort(flat_ids, stable=True).astype(jnp.int32)
    sorted_ids = flat_ids[order]
    token_of = (order // topk).astype(jnp.int32)
    sorted_g = combine.reshape(-1)[order]
    block_rows = min(512, pairs)
    blocks = pairs // block_rows

    def one_block(index):
        start = (index * block_rows).astype(jnp.int32)
        block_ids = lax.dynamic_slice_in_dim(sorted_ids, start, block_rows)
        block_tok = lax.dynamic_slice_in_dim(token_of, start, block_rows)
        block_g = lax.dynamic_slice_in_dim(sorted_g, start, block_rows)
        row_x = tokens[block_tok]
        row_dy = cotangent[block_tok]
        zeros = jnp.zeros((block_rows, width), jnp.float32)

        def per_expert(expert, carry):
            out_acc, grad_acc = carry
            chosen = (block_ids == expert)[:, None]
            out_rows, grad_rows = expert_rows(row_x, row_dy, block_g, w_gate[expert], w_up[expert], w_down[expert])
            return jnp.where(chosen, out_rows, out_acc), jnp.where(chosen, grad_rows, grad_acc)

        return lax.fori_loop(block_ids[0], block_ids[-1] + 1, per_expert, (zeros, zeros))

    out_sorted, grad_sorted = lax.map(one_block, jnp.arange(blocks, dtype=jnp.int32))
    out_pairs = jnp.zeros((pairs, width), jnp.float32).at[order].set(out_sorted.reshape(pairs, width))
    grad_pairs = jnp.zeros((pairs, width), jnp.float32).at[order].set(grad_sorted.reshape(pairs, width))
    out_pairs = out_pairs.reshape(tok_rows, topk, width)
    grad_pairs = grad_pairs.reshape(tok_rows, topk, width)
    mixed = jnp.sum(combine[:, :, None] * out_pairs, axis=1).astype(jnp.bfloat16)
    input_grad = jnp.sum(grad_pairs, axis=1).astype(jnp.bfloat16)
    combine_grad = jnp.sum(out_pairs * cotangent.astype(jnp.float32)[:, None, :], axis=2)
    return mixed, input_grad, combine_grad
```

```python
import functools

import jax
import jax.numpy as jnp
from jax import lax
from jax.experimental import pallas as pl
from jax.experimental.pallas import tpu as pltpu
from jax.sharding import Mesh, PartitionSpec as P

GROUP = ("x", "core")
CHUNK = 128
META = 128
BF, F32 = jnp.bfloat16, jnp.float32


def nn(a, b):
    return jnp.dot(a, b, preferred_element_type=F32)


def nt(a, b):
    return lax.dot_general(a, b, (((1,), (1,)), ((), ())), preferred_element_type=F32)


def tn(a, b):
    return lax.dot_general(a, b, (((0,), (0,)), ((), ())), preferred_element_type=F32)


def pack(tokens, cotangent, routes, combine):
    high = combine.astype(BF)
    low = (combine - high.astype(F32)).astype(BF)
    pad = jnp.zeros((tokens.shape[0], META - 3 * routes.shape[1]), BF)
    return jnp.concatenate([tokens, cotangent, routes.astype(BF), high, low, pad], axis=1)


def experts_kernel(topk, first_ref, t_ref, w_ref, out_ref, rank_ref, acc_ref):
    step = pl.program_id(0)
    local = pl.num_programs(0)
    rows, wide = t_ref.shape
    width = (wide - META) // 2
    first = first_ref[0]
    stride = first_ref[1]

    @pl.when(step == 0)
    def _():
        acc_ref[...] = jnp.zeros_like(acc_ref)
        routes = t_ref[:, 2 * width :].astype(F32).T[:topk]
        masks = []
        for j in range(local):
            name = (first + j * stride).astype(F32)
            masks.append(jnp.max(jnp.where(routes == name, 1.0, 0.0), axis=0, keepdims=True))
        mask = jnp.concatenate(masks, axis=0)
        before = lax.broadcasted_iota(jnp.int32, (rows, rows), 0) < lax.broadcasted_iota(
            jnp.int32, (rows, rows), 1
        )
        rank = nn(mask.astype(BF), jnp.where(before, 1.0, 0.0).astype(BF))
        rank_ref[...] = jnp.where(mask > 0, rank, -1.0)

    rank = rank_ref[pl.ds(step, 1), :]
    count = jnp.max(rank).astype(jnp.int32) + 1
    name = (first + step * stride).astype(F32)
    depth = w_ref.shape[0] * w_ref.shape[3]

    def weight(which):
        return w_ref[:, 0, which].reshape(depth, w_ref.shape[4])

    def chunk(c, carry):
        slot = (lax.broadcasted_iota(jnp.int32, (CHUNK, rows), 0) + c * CHUNK).astype(F32)
        pick = jnp.where(rank == slot, 1.0, 0.0).astype(BF)
        x = nn(pick, t_ref[:, :width]).astype(BF)
        dy = nn(pick, t_ref[:, width : 2 * width]).astype(BF)
        meta = nn(pick, t_ref[:, 2 * width :])
        lane = lax.broadcasted_iota(jnp.int32, meta.shape, 1)
        hit = (meta == name) & (lane < topk)
        both = pltpu.roll(meta, META - topk, 1) + pltpu.roll(meta, META - 2 * topk, 1)
        g = jnp.sum(jnp.where(hit, both, 0.0), axis=1, keepdims=True)
        gate = nn(x, weight(0))
        up = nn(x, weight(1))
        sig = jax.nn.sigmoid(gate)
        silu = gate * sig
        hidden = (silu * up).astype(BF)
        hidden_grad = g * nn(dy, weight(2))
        gate_grad = (hidden_grad * up * sig * (1.0 + gate * (1.0 - sig))).astype(BF)
        up_grad = (hidden_grad * silu).astype(BF)
        eo = nt(hidden, weight(2)).astype(BF).astype(F32)
        grad = (nt(gate_grad, weight(0)) + nt(up_grad, weight(1))).astype(BF)
        cg = jnp.sum(eo * dy.astype(F32), axis=1, keepdims=True)
        cg_high = cg.astype(BF).astype(F32)
        tail = jnp.where(hit, cg_high, 0.0) + pltpu.roll(jnp.where(hit, cg - cg_high, 0.0), topk, 1)
        acc_ref[:, :width] += tn(pick, (g * eo).astype(BF))
        acc_ref[:, width : 2 * width] += tn(pick, grad)
        acc_ref[:, 2 * width :] += tn(pick, tail.astype(BF))
        return carry

    lax.fori_loop(0, (count + CHUNK - 1) // CHUNK, chunk, 0)

    @pl.when(step == local - 1)
    def _():
        out_ref[...] = acc_ref[...].astype(BF)


def experts(first, packed, weights, topk):
    zs, local, three, part, hidden = weights.shape
    rows, wide = packed.shape
    return pl.pallas_call(
        functools.partial(experts_kernel, topk),
        grid_spec=pltpu.PrefetchScalarGridSpec(
            num_scalar_prefetch=1,
            grid=(local,),
            in_specs=[
                pl.BlockSpec((rows, wide), lambda i, s: (0, 0)),
                pl.BlockSpec((zs, 1, three, part, hidden), lambda i, s: (0, i, 0, 0, 0)),
            ],
            out_specs=pl.BlockSpec((rows, wide), lambda i, s: (0, 0)),
            scratch_shapes=[pltpu.VMEM((local, rows), F32), pltpu.VMEM((rows, wide), F32)],
        ),
        out_shape=jax.ShapeDtypeStruct((rows, wide), BF),
        compiler_params=pltpu.CompilerParams(vmem_limit_bytes=56 * 1024 * 1024),
    )(first, packed, weights)


def on_device(tokens, cotangent, routes, combine, w_gate, w_up, w_down):
    rows, width = tokens.shape
    topk = routes.shape[1]
    members = lax.axis_size("x") * lax.axis_size("core")
    shard = jnp.stack([w_gate[0], w_up[0], w_down[0].T])
    weights = lax.all_gather(shard, ("dp", "y"), axis=0)
    weights = weights.reshape((lax.axis_size("dp"), lax.axis_size("y")) + shard.shape)
    packed = lax.all_gather(pack(tokens, cotangent, routes, combine), GROUP, axis=0, tiled=True)
    cores = lax.axis_size("core")
    first = lax.axis_index("x") * lax.axis_size("y") * cores + lax.axis_index("core")
    partial = experts(jnp.stack([first, jnp.full_like(first, cores)]), packed, weights, topk)
    partial = partial.reshape(members, rows, packed.shape[1])
    mine = lax.psum_scatter(partial, GROUP, scatter_dimension=0)
    tail = mine[:, 2 * width :].astype(F32)
    return mine[:, :width], mine[:, width : 2 * width], tail[:, :topk] + tail[:, topk : 2 * topk]


def solution(mesh):
    split = Mesh(mesh.devices.reshape(8, 4, 8, 2), ("dp", "x", "y", "core"))
    owner = ("x", "y", "core")
    token = P(("dp",) + owner, None)
    return jax.shard_map(
        on_device,
        mesh=split,
        in_specs=(token,) * 4 + (P(owner, "dp", None), P(owner, "dp", None), P(owner, None, "dp")),
        out_specs=(token, token, token),
        check_vma=False,
    )
```

```python
import functools

import jax
import jax.numpy as jnp
from jax import lax
from jax.experimental import pallas as pl
from jax.experimental.pallas import tpu as pltpu
from jax.sharding import Mesh, PartitionSpec as P

SIZE = 128
SLOTS = 16
CHUNKS = 16
META = 128
BF, F32 = jnp.bfloat16, jnp.float32


def nn(a, b):
    return jnp.dot(a, b, preferred_element_type=F32)


def nt(a, b):
    return lax.dot_general(a, b, (((1,), (1,)), ((), ())), preferred_element_type=F32)


def tn(a, b):
    return lax.dot_general(a, b, (((0,), (0,)), ((), ())), preferred_element_type=F32)


def pack(tokens, cotangent, routes, combine):
    high = combine.astype(BF)
    low = (combine - high.astype(F32)).astype(BF)
    pad = jnp.zeros((tokens.shape[0], META - 3 * routes.shape[1]), BF)
    return jnp.concatenate([tokens, cotangent, routes.astype(BF), high, low, pad], axis=1)


def route_kernel(topk, first_ref, own_ref, other_ref, rows_ref, pick_ref, table_ref, rank_ref):
    local = rank_ref.shape[1]
    blocks, slots, size = pick_ref.shape
    wide = own_ref.shape[1]
    half = blocks // 2
    before = lax.broadcasted_iota(jnp.int32, (size, size), 0) < lax.broadcasted_iota(
        jnp.int32, (size, size), 1
    )
    before = jnp.where(before, 1.0, 0.0).astype(BF)

    def block(b):
        ref = own_ref if b < half else other_ref
        return ref[(b % half) * size : (b % half + 1) * size]

    for b in range(blocks):
        routes = block(b)[:, wide - META :].astype(F32).T[:topk]
        masks = []
        for j in range(local):
            name = (first_ref[0] + j * first_ref[1]).astype(F32)
            masks.append(jnp.max(jnp.where(routes == name, 1.0, 0.0), axis=0, keepdims=True))
        mask = jnp.concatenate(masks, axis=0)
        rank_ref[b] = jnp.where(mask > 0, nn(mask.astype(BF), before), -1.0)
    bases = [jnp.int32(0)]
    for j in range(local):
        count = jnp.max(rank_ref[:, j]).astype(jnp.int32) + 1
        bases.append(bases[j] + (count + SLOTS - 1) // SLOTS)
    chunks = table_ref.shape[0] - 1
    for q in range(chunks):
        at = jnp.int32(0)
        for j in range(local - 1):
            at += (bases[j + 1] <= q).astype(jnp.int32)
        table_ref[q] = at
    table_ref[chunks] = bases[local]
    slot = lax.broadcasted_iota(jnp.int32, (slots, size), 0)
    for b in range(blocks):
        pick = jnp.zeros((slots, size), F32)
        for j in range(local):
            rank = rank_ref[b, j : j + 1]
            where = rank + (bases[j] * SLOTS).astype(F32)
            pick = jnp.where((where == slot.astype(F32)) & (rank >= 0), 1.0, pick)
        pick = pick.astype(BF)
        pick_ref[b] = pick
        rows_ref[:, b] = nn(pick, block(b)).astype(BF).reshape(chunks, SLOTS, wide)


def experts_kernel(topk, first_ref, table_ref, rows_ref, pick_ref, w_ref, own_ref, other_ref, back_ref):
    q = pl.program_id(0)
    chunks = pl.num_programs(0)
    blocks, slots, size = pick_ref.shape
    wide = rows_ref.shape[3]
    width = (wide - META) // 2
    count = blocks * SLOTS
    depth = w_ref.shape[0] * w_ref.shape[3]

    @pl.when(q >= table_ref[chunks])
    def _():
        back_ref[q] = jnp.zeros(back_ref.shape[1:], BF)

    @pl.when(q < table_ref[chunks])
    def _():
        name = (first_ref[0] + table_ref[q] * first_ref[1]).astype(F32)

        def weight(which):
            return w_ref[:, 0, which].reshape(depth, w_ref.shape[4])

        x = rows_ref[0, :, :, :width].reshape(count, width)
        dy = rows_ref[0, :, :, width : 2 * width].reshape(count, width)
        meta = rows_ref[0, :, :, 2 * width :].astype(F32).reshape(count, META)
        lane = lax.broadcasted_iota(jnp.int32, meta.shape, 1)
        hit = (meta == name) & (lane < topk)
        both = pltpu.roll(meta, META - topk, 1) + pltpu.roll(meta, META - 2 * topk, 1)
        g = jnp.sum(jnp.where(hit, both, 0.0), axis=1, keepdims=True)
        gate = nn(x, weight(0))
        up = nn(x, weight(1))
        sig = jax.nn.sigmoid(gate)
        silu = gate * sig
        hidden = (silu * up).astype(BF)
        hidden_grad = g * nn(dy, weight(2))
        gate_grad = (hidden_grad * up * sig * (1.0 + gate * (1.0 - sig))).astype(BF)
        up_grad = (hidden_grad * silu).astype(BF)
        eo = nt(hidden, weight(2)).astype(BF).astype(F32)
        grad = (nt(gate_grad, weight(0)) + nt(up_grad, weight(1))).astype(BF)
        cg = jnp.sum(eo * dy.astype(F32), axis=1, keepdims=True)
        cg_high = cg.astype(BF).astype(F32)
        tail = jnp.where(hit, cg_high, 0.0) + pltpu.roll(jnp.where(hit, cg - cg_high, 0.0), topk, 1)
        cut = (blocks, SLOTS)
        back_ref[q, :, :, :width] = (g * eo).astype(BF).reshape(cut + (width,))
        back_ref[q, :, :, width : 2 * width] = grad.reshape(cut + (width,))
        back_ref[q, :, :, 2 * width :] = tail.astype(BF).reshape(cut + (META,))

    @pl.when(q == chunks - 1)
    def _():
        half = blocks // 2
        for b in range(blocks):
            ref = own_ref if b < half else other_ref
            at = (b % half) * size
            ref[at : at + size] = tn(pick_ref[b], back_ref[:, b].reshape(slots, wide)).astype(BF)


def route(first, own, other, local, topk):
    half, wide = own.shape
    blocks = 2 * half // SIZE
    vmem = pl.BlockSpec(memory_space=pltpu.VMEM)
    smem = pl.BlockSpec(memory_space=pltpu.SMEM)
    return pl.pallas_call(
        functools.partial(route_kernel, topk),
        in_specs=[smem, vmem, vmem],
        out_specs=[vmem, vmem, smem],
        out_shape=[
            jax.ShapeDtypeStruct((CHUNKS, blocks, SLOTS, wide), BF),
            jax.ShapeDtypeStruct((blocks, CHUNKS * SLOTS, SIZE), BF),
            jax.ShapeDtypeStruct((CHUNKS + 1,), jnp.int32),
        ],
        scratch_shapes=[pltpu.VMEM((blocks, local, SIZE), F32)],
        compiler_params=pltpu.CompilerParams(vmem_limit_bytes=40 * 1024 * 1024),
        cost_estimate=pl.CostEstimate(
            flops=2 * 2 * half * CHUNKS * SLOTS * wide, bytes_accessed=18_000_000, transcendentals=0
        ),
    )(first, own, other)


def experts(first, table, rows, pick, weights, topk):
    zs, local, three, part, hidden = weights.shape
    chunks, blocks, slots, wide = rows.shape
    half = blocks * SIZE // 2
    whole = pl.BlockSpec((half, wide), lambda q, s, t: (0, 0))
    return pl.pallas_call(
        functools.partial(experts_kernel, topk),
        grid_spec=pltpu.PrefetchScalarGridSpec(
            num_scalar_prefetch=2,
            grid=(chunks,),
            in_specs=[
                pl.BlockSpec((1, blocks, slots, wide), lambda q, s, t: (q, 0, 0, 0)),
                pl.BlockSpec(pick.shape, lambda q, s, t: (0, 0, 0)),
                pl.BlockSpec((zs, 1, three, part, hidden), lambda q, s, t: (0, t[q], 0, 0, 0)),
            ],
            out_specs=[whole, whole],
            scratch_shapes=[pltpu.VMEM(rows.shape, BF)],
        ),
        out_shape=[jax.ShapeDtypeStruct((half, wide), BF)] * 2,
        compiler_params=pltpu.CompilerParams(vmem_limit_bytes=48 * 1024 * 1024),
        cost_estimate=pl.CostEstimate(
            flops=2 * 6 * CHUNKS * SIZE * 1024 * hidden, bytes_accessed=36_000_000, transcendentals=0
        ),
    )(first, table, rows, pick, weights)


def shift(array, axis, by):
    size = lax.axis_size(axis)
    return lax.ppermute(array, axis, [(i, (i + by) % size) for i in range(size)])


def gather_group(own):
    middle = own.shape[0] // 2
    left, right = shift(own, "x", 1), shift(own, "x", -1)
    far = [shift(left[:middle], "x", 1), shift(right[middle:], "x", -1)]
    mine = jnp.concatenate([own, right] + far + [left], axis=0)
    return mine, shift(mine, "core", 1)


def add(a, b):
    return (a.astype(F32) + b.astype(F32)).astype(BF)


def sum_group(mine, other):
    total = add(mine, shift(other, "core", 1))
    size = total.shape[0] // 4
    middle = size // 2
    part = [total[o * size : (o + 1) * size] for o in range(4)]
    from_left = shift(part[2][:middle], "x", 1)
    from_right = shift(part[2][middle:], "x", -1)
    to_right = jnp.concatenate([add(part[1][:middle], from_left), part[1][middle:]], axis=0)
    to_left = jnp.concatenate([part[3][:middle], add(part[3][middle:], from_right)], axis=0)
    return part[0].astype(F32) + shift(to_right, "x", 1).astype(F32) + shift(to_left, "x", -1).astype(F32)


def on_device(tokens, cotangent, routes, combine, w_gate, w_up, w_down):
    width = tokens.shape[1]
    topk = routes.shape[1]
    shard = jnp.stack([w_gate[0], w_up[0], w_down[0].T])
    weights = lax.all_gather(shard, ("dp", "y"), axis=0)
    weights = weights.reshape((lax.axis_size("dp"), lax.axis_size("y")) + shard.shape)
    mine, other = gather_group(pack(tokens, cotangent, routes, combine))
    cores = lax.axis_size("core")
    first = lax.axis_index("x") * lax.axis_size("y") * cores + lax.axis_index("core")
    first = jnp.stack([first, jnp.full_like(first, cores)])
    rows, pick, table = route(first, mine, other, weights.shape[1], topk)
    total = sum_group(*experts(first, table, rows, pick, weights, topk))
    tail = total[:, 2 * width :]
    return (
        total[:, :width].astype(BF),
        total[:, width : 2 * width].astype(BF),
        tail[:, :topk] + tail[:, topk : 2 * topk],
    )


def solution(mesh):
    split = Mesh(mesh.devices.reshape(8, 4, 8, 2), ("dp", "x", "y", "core"))
    owner = ("x", "y", "core")
    token = P(("dp",) + owner, None)
    return jax.shard_map(
        on_device,
        mesh=split,
        in_specs=(token,) * 4 + (P(owner, "dp", None), P(owner, "dp", None), P(owner, None, "dp")),
        out_specs=(token, token, token),
        check_vma=False,
    )
```

```python
import functools

import jax
import jax.numpy as jnp
from jax import lax
from jax.experimental import pallas as pl
from jax.experimental.pallas import tpu as pltpu
from jax.sharding import Mesh, PartitionSpec as P

SIZE = 128
SLOTS = 16
CHUNKS = 16
META = 128
BF, F32 = jnp.bfloat16, jnp.float32


def nn(a, b):
    return jnp.dot(a, b, preferred_element_type=F32)


def nt(a, b):
    return lax.dot_general(a, b, (((1,), (1,)), ((), ())), preferred_element_type=F32)


def tn(a, b):
    return lax.dot_general(a, b, (((0,), (0,)), ((), ())), preferred_element_type=F32)


def pack(tokens, cotangent, routes, combine):
    high = combine.astype(BF)
    low = (combine - high.astype(F32)).astype(BF)
    pad = jnp.zeros((tokens.shape[0], META - 3 * routes.shape[1]), BF)
    return jnp.concatenate([tokens, cotangent, routes.astype(BF), high, low, pad], axis=1)


def route_kernel(topk, first_ref, own_ref, other_ref, rows_ref, pick_ref, table_ref, rank_ref):
    local = rank_ref.shape[1]
    blocks, slots, size = pick_ref.shape
    wide = own_ref.shape[1]
    half = blocks // 2
    before = lax.broadcasted_iota(jnp.int32, (size, size), 0) < lax.broadcasted_iota(
        jnp.int32, (size, size), 1
    )
    before = jnp.where(before, 1.0, 0.0).astype(BF)

    def block(b):
        ref = own_ref if b < half else other_ref
        return ref[(b % half) * size : (b % half + 1) * size]

    for b in range(blocks):
        routes = block(b)[:, wide - META :].astype(F32).T[:topk]
        masks = []
        for j in range(local):
            name = (first_ref[0] + j * first_ref[1]).astype(F32)
            masks.append(jnp.max(jnp.where(routes == name, 1.0, 0.0), axis=0, keepdims=True))
        mask = jnp.concatenate(masks, axis=0)
        rank_ref[b] = jnp.where(mask > 0, nn(mask.astype(BF), before), -1.0)
    bases = [jnp.int32(0)]
    for j in range(local):
        count = jnp.max(rank_ref[:, j]).astype(jnp.int32) + 1
        bases.append(bases[j] + (count + SLOTS - 1) // SLOTS)
    chunks = table_ref.shape[0] - 1
    for q in range(chunks):
        at = jnp.int32(0)
        for j in range(local - 1):
            at += (bases[j + 1] <= q).astype(jnp.int32)
        table_ref[q] = at
    table_ref[chunks] = bases[local]
    slot = lax.broadcasted_iota(jnp.int32, (slots, size), 0)
    for b in range(blocks):
        pick = jnp.zeros((slots, size), F32)
        for j in range(local):
            rank = rank_ref[b, j : j + 1]
            where = rank + (bases[j] * SLOTS).astype(F32)
            pick = jnp.where((where == slot.astype(F32)) & (rank >= 0), 1.0, pick)
        pick = pick.astype(BF)
        pick_ref[b] = pick
        rows_ref[:, b] = nn(pick, block(b)).astype(BF).reshape(chunks, SLOTS, wide)


def experts_kernel(topk, first_ref, table_ref, rows_ref, pick_ref, w_ref, own_ref, other_ref, back_ref):
    q = pl.program_id(0)
    chunks = pl.num_programs(0)
    blocks, slots, size = pick_ref.shape
    wide = rows_ref.shape[3]
    width = (wide - META) // 2
    count = blocks * SLOTS
    zs, part = w_ref.shape[0], w_ref.shape[2]
    hidden_units = w_ref.shape[3] // 3

    @pl.when(q >= table_ref[chunks])
    def _():
        back_ref[q] = jnp.zeros(back_ref.shape[1:], BF)

    @pl.when(q < table_ref[chunks])
    def _():
        name = (first_ref[0] + table_ref[q] * first_ref[1]).astype(F32)

        gate_up = w_ref[:, 0, :, : 2 * hidden_units].reshape(zs * part, 2 * hidden_units)
        down = jnp.concatenate(
            [
                jnp.concatenate([w_ref[z, 0, :, at : at + META] for z in range(zs)], axis=1)
                for at in range(2 * hidden_units, 3 * hidden_units, META)
            ],
            axis=0,
        )
        x = rows_ref[0, :, :, :width].reshape(count, width)
        dy = rows_ref[0, :, :, width : 2 * width].reshape(count, width)
        meta = rows_ref[0, :, :, 2 * width :].astype(F32).reshape(count, META)
        lane = lax.broadcasted_iota(jnp.int32, meta.shape, 1)
        hit = (meta == name) & (lane < topk)
        both = pltpu.roll(meta, META - topk, 1) + pltpu.roll(meta, META - 2 * topk, 1)
        g = jnp.sum(jnp.where(hit, both, 0.0), axis=1, keepdims=True)
        pre = nn(x, gate_up)
        gate, up = pre[:, :hidden_units], pre[:, hidden_units:]
        sig = jax.nn.sigmoid(gate)
        silu = gate * sig
        hidden = (silu * up).astype(BF)
        hidden_grad = g * nt(dy, down)
        gate_grad = (hidden_grad * up * sig * (1.0 + gate * (1.0 - sig))).astype(BF)
        up_grad = (hidden_grad * silu).astype(BF)
        eo = nn(hidden, down).astype(BF).astype(F32)
        grad = (nt(jnp.concatenate([gate_grad, up_grad], axis=1), gate_up)).astype(BF)
        cg = jnp.sum(eo * dy.astype(F32), axis=1, keepdims=True)
        cg_high = cg.astype(BF).astype(F32)
        tail = jnp.where(hit, cg_high, 0.0) + pltpu.roll(jnp.where(hit, cg - cg_high, 0.0), topk, 1)
        cut = (blocks, SLOTS)
        back_ref[q, :, :, :width] = (g * eo).astype(BF).reshape(cut + (width,))
        back_ref[q, :, :, width : 2 * width] = grad.reshape(cut + (width,))
        back_ref[q, :, :, 2 * width :] = tail.astype(BF).reshape(cut + (META,))

    @pl.when(q == chunks - 1)
    def _():
        half = blocks // 2
        for b in range(blocks):
            ref = own_ref if b < half else other_ref
            at = lax.rem(first_ref[2] + b % half, half) * size
            ref[pl.ds(pl.multiple_of(at, size), size)] = tn(pick_ref[b], back_ref[:, b].reshape(slots, wide)).astype(BF)


def route(first, own, other, local, topk):
    half, wide = own.shape
    blocks = 2 * half // SIZE
    vmem = pl.BlockSpec(memory_space=pltpu.VMEM)
    smem = pl.BlockSpec(memory_space=pltpu.SMEM)
    return pl.pallas_call(
        functools.partial(route_kernel, topk),
        in_specs=[smem, vmem, vmem],
        out_specs=[vmem, vmem, smem],
        out_shape=[
            jax.ShapeDtypeStruct((CHUNKS, blocks, SLOTS, wide), BF),
            jax.ShapeDtypeStruct((blocks, CHUNKS * SLOTS, SIZE), BF),
            jax.ShapeDtypeStruct((CHUNKS + 1,), jnp.int32),
        ],
        scratch_shapes=[pltpu.VMEM((blocks, local, SIZE), F32)],
        compiler_params=pltpu.CompilerParams(vmem_limit_bytes=40 * 1024 * 1024),
        cost_estimate=pl.CostEstimate(
            flops=2 * 2 * half * CHUNKS * SLOTS * wide, bytes_accessed=18_000_000, transcendentals=0
        ),
    )(first, own, other)


def experts(first, table, rows, pick, weights, topk):
    zs, local, part, hidden = weights.shape
    chunks, blocks, slots, wide = rows.shape
    half = blocks * SIZE // 2
    whole = pl.BlockSpec((half, wide), lambda q, s, t: (0, 0))
    return pl.pallas_call(
        functools.partial(experts_kernel, topk),
        grid_spec=pltpu.PrefetchScalarGridSpec(
            num_scalar_prefetch=2,
            grid=(chunks,),
            in_specs=[
                pl.BlockSpec((1, blocks, slots, wide), lambda q, s, t: (jnp.minimum(q, t[chunks] - 1), 0, 0, 0)),
                pl.BlockSpec(pick.shape, lambda q, s, t: (0, 0, 0)),
                pl.BlockSpec((zs, 1, part, hidden), lambda q, s, t: (0, t[q], 0, 0)),
            ],
            out_specs=[whole, whole],
            scratch_shapes=[pltpu.VMEM(rows.shape, BF)],
        ),
        out_shape=[jax.ShapeDtypeStruct((half, wide), BF)] * 2,
        compiler_params=pltpu.CompilerParams(vmem_limit_bytes=48 * 1024 * 1024),
        cost_estimate=pl.CostEstimate(
            flops=2 * 2 * CHUNKS * SIZE * 1024 * hidden, bytes_accessed=36_000_000, transcendentals=0
        ),
    )(first, table, rows, pick, weights)


def shift(array, axis, by):
    size = lax.axis_size(axis)
    return lax.ppermute(array, axis, [(i, (i + by) % size) for i in range(size)])


def gather_group(own):
    middle = own.shape[0] // 2
    left, right = shift(own, "x", 1), shift(own, "x", -1)
    far = [shift(left[:middle], "x", 1), shift(right[middle:], "x", -1)]
    mine = jnp.concatenate([own, right] + far + [left], axis=0)
    return mine, shift(mine, "core", 1)


def add(a, b):
    return (a.astype(F32) + b.astype(F32)).astype(BF)


def sum_group(mine, other):
    size = lax.axis_size("x")
    total = add(mine, shift(other, "core", 1)).reshape((size, mine.shape[0] // size, mine.shape[1]))
    parts = lax.all_to_all(total, "x", 0, 0, tiled=True)
    return jnp.sum(parts.astype(F32), axis=0)


def on_device(tokens, cotangent, routes, combine, w_gate, w_up, w_down):
    width = tokens.shape[1]
    topk = routes.shape[1]
    down = w_down[0]
    cuts = [down[at : at + META] for at in range(0, down.shape[0], META)]
    shard = jnp.concatenate([w_gate[0], w_up[0]] + cuts, axis=1)
    weights = lax.all_gather(shard, ("dp", "y"), axis=0)
    weights = weights.reshape((lax.axis_size("dp"), lax.axis_size("y")) + shard.shape)
    mine, other = gather_group(pack(tokens, cotangent, routes, combine))
    cores = lax.axis_size("core")
    first = lax.axis_index("x") * lax.axis_size("y") * cores + lax.axis_index("core")
    first = jnp.stack([first, jnp.full_like(first, cores), lax.axis_index("x")])
    rows, pick, table = route(first, mine, other, weights.shape[1], topk)
    total = sum_group(*experts(first, table, rows, pick, weights, topk))
    tail = total[:, 2 * width :]
    return (
        total[:, :width].astype(BF),
        total[:, width : 2 * width].astype(BF),
        tail[:, :topk] + tail[:, topk : 2 * topk],
    )


def solution(mesh):
    split = Mesh(mesh.devices.reshape(8, 4, 8, 2), ("dp", "x", "y", "core"))
    owner = ("x", "y", "core")
    token = P(("dp",) + owner, None)
    return jax.shard_map(
        on_device,
        mesh=split,
        in_specs=(token,) * 4 + (P(owner, "dp", None), P(owner, "dp", None), P(owner, None, "dp")),
        out_specs=(token, token, token),
        check_vma=False,
    )
```

```python
import functools

import jax
import jax.numpy as jnp
from jax import lax
from jax.experimental import pallas as pl
from jax.experimental.pallas import tpu as pltpu
from jax.sharding import Mesh, PartitionSpec as P

SIZE = 128
SLOTS = 16
CHUNKS = 14
META = 128
BF, F32 = jnp.bfloat16, jnp.float32


def nn(a, b):
    return jnp.dot(a, b, preferred_element_type=F32)


def nt(a, b):
    return lax.dot_general(a, b, (((1,), (1,)), ((), ())), preferred_element_type=F32)


def tn(a, b):
    return lax.dot_general(a, b, (((0,), (0,)), ((), ())), preferred_element_type=F32)


def pack(tokens, cotangent, routes, combine):
    high = combine.astype(BF)
    low = (combine - high.astype(F32)).astype(BF)
    pad = jnp.zeros((tokens.shape[0], META - 3 * routes.shape[1]), BF)
    return jnp.concatenate([tokens, cotangent, routes.astype(BF), high, low, pad], axis=1)


def route_kernel(topk, first_ref, own_ref, other_ref, rows_ref, pick_ref, table_ref, rank_ref):
    local = rank_ref.shape[1]
    blocks, slots, size = pick_ref.shape
    wide = own_ref.shape[1]
    half = blocks // 2
    before = lax.broadcasted_iota(jnp.int32, (size, size), 0) < lax.broadcasted_iota(
        jnp.int32, (size, size), 1
    )
    before = jnp.where(before, 1.0, 0.0).astype(BF)

    def block(b):
        ref = own_ref if b < half else other_ref
        return ref[(b % half) * size : (b % half + 1) * size]

    for b in range(blocks):
        routes = block(b)[:, wide - META :].astype(F32).T[:topk]
        masks = []
        for j in range(local):
            name = (first_ref[0] + j * first_ref[1]).astype(F32)
            masks.append(jnp.max(jnp.where(routes == name, 1.0, 0.0), axis=0, keepdims=True))
        mask = jnp.concatenate(masks, axis=0)
        rank_ref[b] = jnp.where(mask > 0, nn(mask.astype(BF), before), -1.0)
    bases = [jnp.int32(0)]
    for j in range(local):
        count = jnp.max(rank_ref[:, j]).astype(jnp.int32) + 1
        bases.append(bases[j] + (count + SLOTS - 1) // SLOTS)
    chunks = table_ref.shape[0] - 1
    for q in range(chunks):
        at = jnp.int32(0)
        for j in range(local - 1):
            at += (bases[j + 1] <= q).astype(jnp.int32)
        table_ref[q] = at
    table_ref[chunks] = bases[local]
    slot = lax.broadcasted_iota(jnp.int32, (slots, size), 0)
    for b in range(blocks):
        pick = jnp.zeros((slots, size), F32)
        for j in range(local):
            rank = rank_ref[b, j : j + 1]
            where = rank + (bases[j] * SLOTS).astype(F32)
            pick = jnp.where((where == slot.astype(F32)) & (rank >= 0), 1.0, pick)
        pick = pick.astype(BF)
        pick_ref[b] = pick
        rows_ref[:, b] = nn(pick, block(b)).astype(BF).reshape(chunks, SLOTS, wide)


def experts_kernel(topk, first_ref, table_ref, rows_ref, pick_ref, w_ref, own_ref, other_ref, back_ref):
    q = pl.program_id(0)
    chunks = pl.num_programs(0)
    blocks, slots, size = pick_ref.shape
    wide = rows_ref.shape[3]
    width = (wide - META) // 2
    count = blocks * SLOTS
    zs, part = w_ref.shape[0], w_ref.shape[2]
    hidden_units = w_ref.shape[3] // 3

    @pl.when(q >= table_ref[chunks])
    def _():
        back_ref[q] = jnp.zeros(back_ref.shape[1:], BF)

    @pl.when(q < table_ref[chunks])
    def _():
        name = (first_ref[0] + table_ref[q] * first_ref[1]).astype(F32)

        gate_up = w_ref[:, 0, :, : 2 * hidden_units].reshape(zs * part, 2 * hidden_units)
        down = jnp.concatenate(
            [
                jnp.concatenate([w_ref[z, 0, :, at : at + META] for z in range(zs)], axis=1)
                for at in range(2 * hidden_units, 3 * hidden_units, META)
            ],
            axis=0,
        )
        x = rows_ref[0, :, :, :width].reshape(count, width)
        dy = rows_ref[0, :, :, width : 2 * width].reshape(count, width)
        meta = rows_ref[0, :, :, 2 * width :].astype(F32).reshape(count, META)
        lane = lax.broadcasted_iota(jnp.int32, meta.shape, 1)
        hit = (meta == name) & (lane < topk)
        both = pltpu.roll(meta, META - topk, 1) + pltpu.roll(meta, META - 2 * topk, 1)
        g = jnp.sum(jnp.where(hit, both, 0.0), axis=1, keepdims=True)
        pre = nn(x, gate_up)
        gate, up = pre[:, :hidden_units], pre[:, hidden_units:]
        sig = jax.nn.sigmoid(gate)
        silu = gate * sig
        hidden = (silu * up).astype(BF)
        hidden_grad = g * nt(dy, down)
        gate_grad = (hidden_grad * up * sig * (1.0 + gate * (1.0 - sig))).astype(BF)
        up_grad = (hidden_grad * silu).astype(BF)
        eo = nn(hidden, down).astype(BF).astype(F32)
        grad = (nt(jnp.concatenate([gate_grad, up_grad], axis=1), gate_up)).astype(BF)
        cg = jnp.sum(eo * dy.astype(F32), axis=1, keepdims=True)
        cg_high = cg.astype(BF).astype(F32)
        tail = jnp.where(hit, cg_high, 0.0) + pltpu.roll(jnp.where(hit, cg - cg_high, 0.0), topk, 1)
        cut = (blocks, SLOTS)
        back_ref[q, :, :, :width] = (g * eo).astype(BF).reshape(cut + (width,))
        back_ref[q, :, :, width : 2 * width] = grad.reshape(cut + (width,))
        back_ref[q, :, :, 2 * width :] = tail.astype(BF).reshape(cut + (META,))

    @pl.when(q == chunks - 1)
    def _():
        half = blocks // 2
        for b in range(blocks):
            ref = own_ref if b < half else other_ref
            at = lax.rem(first_ref[2] + b % half, half) * size
            ref[pl.ds(pl.multiple_of(at, size), size)] = tn(pick_ref[b], back_ref[:, b].reshape(slots, wide)).astype(BF)


def route(first, own, other, local, topk):
    half, wide = own.shape
    blocks = 2 * half // SIZE
    vmem = pl.BlockSpec(memory_space=pltpu.VMEM)
    smem = pl.BlockSpec(memory_space=pltpu.SMEM)
    return pl.pallas_call(
        functools.partial(route_kernel, topk),
        in_specs=[smem, vmem, vmem],
        out_specs=[vmem, vmem, smem],
        out_shape=[
            jax.ShapeDtypeStruct((CHUNKS, blocks, SLOTS, wide), BF),
            jax.ShapeDtypeStruct((blocks, CHUNKS * SLOTS, SIZE), BF),
            jax.ShapeDtypeStruct((CHUNKS + 1,), jnp.int32),
        ],
        scratch_shapes=[pltpu.VMEM((blocks, local, SIZE), F32)],
        compiler_params=pltpu.CompilerParams(vmem_limit_bytes=40 * 1024 * 1024),
        cost_estimate=pl.CostEstimate(
            flops=2 * 2 * half * CHUNKS * SLOTS * wide, bytes_accessed=18_000_000, transcendentals=0
        ),
    )(first, own, other)


def experts(first, table, rows, pick, weights, topk):
    zs, local, part, hidden = weights.shape
    chunks, blocks, slots, wide = rows.shape
    half = blocks * SIZE // 2
    whole = pl.BlockSpec((half, wide), lambda q, s, t: (0, 0))
    return pl.pallas_call(
        functools.partial(experts_kernel, topk),
        grid_spec=pltpu.PrefetchScalarGridSpec(
            num_scalar_prefetch=2,
            grid=(chunks,),
            in_specs=[
                pl.BlockSpec((1, blocks, slots, wide), lambda q, s, t: (jnp.minimum(q, t[chunks] - 1), 0, 0, 0)),
                pl.BlockSpec(pick.shape, lambda q, s, t: (0, 0, 0)),
                pl.BlockSpec((zs, 1, part, hidden), lambda q, s, t: (0, t[q], 0, 0)),
            ],
            out_specs=[whole, whole],
            scratch_shapes=[pltpu.VMEM(rows.shape, BF)],
        ),
        out_shape=[jax.ShapeDtypeStruct((half, wide), BF)] * 2,
        compiler_params=pltpu.CompilerParams(vmem_limit_bytes=48 * 1024 * 1024),
        cost_estimate=pl.CostEstimate(
            flops=2 * 2 * CHUNKS * SIZE * 1024 * hidden, bytes_accessed=36_000_000, transcendentals=0
        ),
    )(first, table, rows, pick, weights)


def shift(array, axis, by):
    size = lax.axis_size(axis)
    return lax.ppermute(array, axis, [(i, (i + by) % size) for i in range(size)])


def gather_group(own):
    middle = own.shape[0] // 2
    left, right = shift(own, "x", 1), shift(own, "x", -1)
    far = [shift(left[:middle], "x", 1), shift(right[middle:], "x", -1)]
    mine = jnp.concatenate([own, right] + far + [left], axis=0)
    return mine, shift(mine, "core", 1)


def add(a, b):
    return (a.astype(F32) + b.astype(F32)).astype(BF)


def sum_group(mine, other):
    size = lax.axis_size("x")
    total = add(mine, shift(other, "core", 1)).reshape((size, mine.shape[0] // size, mine.shape[1]))
    parts = lax.all_to_all(total, "x", 0, 0, tiled=True)
    return jnp.sum(parts.astype(F32), axis=0)


def shard_kernel(gate_ref, up_ref, down_ref, out_ref):
    units, lanes = down_ref.shape[1:]
    out_ref[:, :units] = gate_ref[0]
    out_ref[:, units : 2 * units] = up_ref[0]
    for at in range(0, units, lanes):
        out_ref[:, 2 * units + at : 2 * units + at + lanes] = down_ref[0, at : at + lanes]


def pack_shard(w_gate, w_up, w_down):
    part, units = w_gate.shape[1:]
    return pl.pallas_call(
        shard_kernel,
        in_specs=[pl.BlockSpec(memory_space=pltpu.VMEM)] * 3,
        out_specs=pl.BlockSpec(memory_space=pltpu.VMEM),
        out_shape=jax.ShapeDtypeStruct((part, 3 * units), BF),
    )(w_gate, w_up, w_down)


def on_device(tokens, cotangent, routes, combine, w_gate, w_up, w_down):
    width = tokens.shape[1]
    topk = routes.shape[1]
    shard = pack_shard(w_gate, w_up, w_down)
    weights = lax.all_gather(shard, ("dp", "y"), axis=0)
    weights = weights.reshape((lax.axis_size("dp"), lax.axis_size("y")) + shard.shape)
    mine, other = gather_group(pack(tokens, cotangent, routes, combine))
    cores = lax.axis_size("core")
    first = lax.axis_index("x") * lax.axis_size("y") * cores + lax.axis_index("core")
    first = jnp.stack([first, jnp.full_like(first, cores), lax.axis_index("x")])
    rows, pick, table = route(first, mine, other, weights.shape[1], topk)
    total = sum_group(*experts(first, table, rows, pick, weights, topk))
    tail = total[:, 2 * width :]
    return (
        total[:, :width].astype(BF),
        total[:, width : 2 * width].astype(BF),
        tail[:, :topk] + tail[:, topk : 2 * topk],
    )


def solution(mesh):
    split = Mesh(mesh.devices.reshape(8, 4, 8, 2), ("dp", "x", "y", "core"))
    owner = ("x", "y", "core")
    token = P(("dp",) + owner, None)
    return jax.shard_map(
        on_device,
        mesh=split,
        in_specs=(token,) * 4 + (P(owner, "dp", None), P(owner, "dp", None), P(owner, None, "dp")),
        out_specs=(token, token, token),
        check_vma=False,
    )
```

```python
import functools

import jax
import jax.numpy as jnp
from jax import lax
from jax.experimental import pallas as pl
from jax.experimental.pallas import tpu as pltpu
from jax.sharding import Mesh, PartitionSpec as P

SIZE = 128
SLOTS = 16
CHUNKS = 14
META = 128
BF, F32 = jnp.bfloat16, jnp.float32


def nn(a, b):
    return jnp.dot(a, b, preferred_element_type=F32)


def nt(a, b):
    return lax.dot_general(a, b, (((1,), (1,)), ((), ())), preferred_element_type=F32)


def tn(a, b):
    return lax.dot_general(a, b, (((0,), (0,)), ((), ())), preferred_element_type=F32)


def pack(tokens, cotangent, routes, combine):
    high = combine.astype(BF)
    low = (combine - high.astype(F32)).astype(BF)
    pad = jnp.zeros((tokens.shape[0], META - 3 * routes.shape[1]), BF)
    return jnp.concatenate([tokens, cotangent, routes.astype(BF), high, low, pad], axis=1)


def route_kernel(topk, first_ref, own_ref, other_ref, rows_ref, pick_ref, table_ref, rank_ref):
    local = rank_ref.shape[1]
    blocks, slots, size = pick_ref.shape
    wide = own_ref.shape[1]
    half = blocks // 2
    before = lax.broadcasted_iota(jnp.int32, (size, size), 0) < lax.broadcasted_iota(
        jnp.int32, (size, size), 1
    )
    before = jnp.where(before, 1.0, 0.0).astype(BF)

    def block(b):
        ref = own_ref if b < half else other_ref
        return ref[(b % half) * size : (b % half + 1) * size]

    for b in range(blocks):
        routes = block(b)[:, wide - META :].astype(F32).T[:topk]
        masks = []
        for j in range(local):
            name = (first_ref[0] + j * first_ref[1]).astype(F32)
            masks.append(jnp.max(jnp.where(routes == name, 1.0, 0.0), axis=0, keepdims=True))
        mask = jnp.concatenate(masks, axis=0)
        rank_ref[b] = jnp.where(mask > 0, nn(mask.astype(BF), before), -1.0)
    bases = [jnp.int32(0)]
    for j in range(local):
        count = jnp.max(rank_ref[:, j]).astype(jnp.int32) + 1
        bases.append(bases[j] + (count + SLOTS - 1) // SLOTS)
    chunks = pick_ref.shape[1] // SLOTS
    ahead = jnp.int32(0)
    for q in range(chunks):
        at, start, end = jnp.int32(0), bases[0], bases[1]
        for j in range(1, local):
            past = bases[j] <= q
            at += past.astype(jnp.int32)
            start = jnp.where(past, bases[j], start)
            end = jnp.where(past, bases[j + 1], end)
        odd = lax.rem(q - start, 2)
        pair = (odd == 0) & (end - q >= 2)
        ahead = jnp.where(pair, jnp.int32(min(q + 1, chunks - 1)), ahead)
        table_ref[q] = at
        table_ref[chunks + 1 + q] = jnp.where(pair, 2, 1 - odd)
        table_ref[2 * chunks + 1 + q] = ahead
    table_ref[chunks] = jnp.minimum(bases[local], chunks)
    slot = lax.broadcasted_iota(jnp.int32, (slots, size), 0)
    for b in range(blocks):
        pick = jnp.zeros((slots, size), F32)
        for j in range(local):
            rank = rank_ref[b, j : j + 1]
            where = rank + (bases[j] * SLOTS).astype(F32)
            pick = jnp.where((where == slot.astype(F32)) & (rank >= 0), 1.0, pick)
        pick = pick.astype(BF)
        pick_ref[b] = pick
        rows_ref[:, b] = nn(pick, block(b)).astype(BF).reshape(chunks, SLOTS, wide)


def experts_kernel(topk, first_ref, table_ref, rows_ref, next_ref, pick_ref, w_ref, own_ref, other_ref, back_ref):
    q = pl.program_id(0)
    chunks = pl.num_programs(0)
    blocks, slots, size = pick_ref.shape
    wide = rows_ref.shape[3]
    width = (wide - META) // 2
    zs, part = w_ref.shape[0], w_ref.shape[2]
    hidden_units = w_ref.shape[3] // 3

    @pl.when(q >= table_ref[chunks])
    def _():
        back_ref[q] = jnp.zeros(back_ref.shape[1:], BF)

    def compute(*refs):
        count = len(refs) * blocks * SLOTS

        def lanes(at, size):
            return jnp.concatenate([ref[0, :, :, at : at + size] for ref in refs], axis=0).reshape(count, size)

        name = (first_ref[0] + table_ref[q] * first_ref[1]).astype(F32)

        gate_up = w_ref[:, 0, :, : 2 * hidden_units].reshape(zs * part, 2 * hidden_units)
        down = jnp.concatenate(
            [
                jnp.concatenate([w_ref[z, 0, :, at : at + META] for z in range(zs)], axis=1)
                for at in range(2 * hidden_units, 3 * hidden_units, META)
            ],
            axis=0,
        )
        x = lanes(0, width)
        dy = lanes(width, width)
        meta = lanes(2 * width, META).astype(F32)
        lane = lax.broadcasted_iota(jnp.int32, meta.shape, 1)
        hit = (meta == name) & (lane < topk)
        both = pltpu.roll(meta, META - topk, 1) + pltpu.roll(meta, META - 2 * topk, 1)
        g = jnp.sum(jnp.where(hit, both, 0.0), axis=1, keepdims=True)
        pre = nn(x, gate_up)
        gate, up = pre[:, :hidden_units], pre[:, hidden_units:]
        sig = jax.nn.sigmoid(gate)
        silu = gate * sig
        hidden = (silu * up).astype(BF)
        hidden_grad = g * nt(dy, down)
        gate_grad = (hidden_grad * up * sig * (1.0 + gate * (1.0 - sig))).astype(BF)
        up_grad = (hidden_grad * silu).astype(BF)
        eo = nn(hidden, down).astype(BF).astype(F32)
        grad = (nt(jnp.concatenate([gate_grad, up_grad], axis=1), gate_up)).astype(BF)
        cg = jnp.sum(eo * dy.astype(F32), axis=1, keepdims=True)
        cg_high = cg.astype(BF).astype(F32)
        tail = jnp.where(hit, cg_high, 0.0) + pltpu.roll(jnp.where(hit, cg - cg_high, 0.0), topk, 1)
        cut = (len(refs), blocks, SLOTS)
        mixed = (g * eo).astype(BF).reshape(cut + (width,))
        grad = grad.reshape(cut + (width,))
        tail = tail.astype(BF).reshape(cut + (META,))
        for i in range(len(refs)):
            back_ref[q + i, :, :, :width] = mixed[i]
            back_ref[q + i, :, :, width : 2 * width] = grad[i]
            back_ref[q + i, :, :, 2 * width :] = tail[i]

    kind = table_ref[chunks + 1 + q]

    @pl.when((q < table_ref[chunks]) & (kind == 1))
    def _():
        compute(rows_ref)

    @pl.when((q < table_ref[chunks] - 1) & (kind == 2))
    def _():
        compute(rows_ref, next_ref)

    @pl.when(q == chunks - 1)
    def _():
        half = blocks // 2
        for b in range(blocks):
            ref = own_ref if b < half else other_ref
            at = lax.rem(first_ref[2] + b % half, half) * size
            ref[pl.ds(pl.multiple_of(at, size), size)] = tn(pick_ref[b], back_ref[:, b].reshape(slots, wide)).astype(BF)


def route(first, own, other, local, topk):
    half, wide = own.shape
    blocks = 2 * half // SIZE
    vmem = pl.BlockSpec(memory_space=pltpu.VMEM)
    smem = pl.BlockSpec(memory_space=pltpu.SMEM)
    return pl.pallas_call(
        functools.partial(route_kernel, topk),
        in_specs=[smem, vmem, vmem],
        out_specs=[vmem, vmem, smem],
        out_shape=[
            jax.ShapeDtypeStruct((CHUNKS, blocks, SLOTS, wide), BF),
            jax.ShapeDtypeStruct((blocks, CHUNKS * SLOTS, SIZE), BF),
            jax.ShapeDtypeStruct((3 * CHUNKS + 1,), jnp.int32),
        ],
        scratch_shapes=[pltpu.VMEM((blocks, local, SIZE), F32)],
        compiler_params=pltpu.CompilerParams(vmem_limit_bytes=40 * 1024 * 1024),
        cost_estimate=pl.CostEstimate(
            flops=2 * 2 * half * CHUNKS * SLOTS * wide, bytes_accessed=18_000_000, transcendentals=0
        ),
    )(first, own, other)


def experts(first, table, rows, pick, weights, topk):
    zs, local, part, hidden = weights.shape
    chunks, blocks, slots, wide = rows.shape
    half = blocks * SIZE // 2
    whole = pl.BlockSpec((half, wide), lambda q, s, t: (0, 0))
    return pl.pallas_call(
        functools.partial(experts_kernel, topk),
        grid_spec=pltpu.PrefetchScalarGridSpec(
            num_scalar_prefetch=2,
            grid=(chunks,),
            in_specs=[
                pl.BlockSpec((1, blocks, slots, wide), lambda q, s, t: (jnp.minimum(q, t[chunks] - 1), 0, 0, 0)),
                pl.BlockSpec((1, blocks, slots, wide), lambda q, s, t: (t[2 * chunks + 1 + q], 0, 0, 0)),
                pl.BlockSpec(pick.shape, lambda q, s, t: (0, 0, 0)),
                pl.BlockSpec((zs, 1, part, hidden), lambda q, s, t: (0, t[q], 0, 0)),
            ],
            out_specs=[whole, whole],
            scratch_shapes=[pltpu.VMEM(rows.shape, BF)],
        ),
        out_shape=[jax.ShapeDtypeStruct((half, wide), BF)] * 2,
        compiler_params=pltpu.CompilerParams(vmem_limit_bytes=48 * 1024 * 1024),
        cost_estimate=pl.CostEstimate(
            flops=2 * 2 * CHUNKS * SIZE * 1024 * hidden, bytes_accessed=36_000_000, transcendentals=0
        ),
    )(first, table, rows, rows, pick, weights)


def shift(array, axis, by):
    size = lax.axis_size(axis)
    return lax.ppermute(array, axis, [(i, (i + by) % size) for i in range(size)])


def gather_group(own):
    middle = own.shape[0] // 2
    left, right = shift(own, "x", 1), shift(own, "x", -1)
    far = [shift(left[:middle], "x", 1), shift(right[middle:], "x", -1)]
    mine = jnp.concatenate([own, right] + far + [left], axis=0)
    return mine, shift(mine, "core", 1)


def add(a, b):
    return (a.astype(F32) + b.astype(F32)).astype(BF)


def sum_group(mine, other):
    size = lax.axis_size("x")
    total = add(mine, shift(other, "core", 1)).reshape((size, mine.shape[0] // size, mine.shape[1]))
    parts = lax.all_to_all(total, "x", 0, 0, tiled=True)
    return jnp.sum(parts.astype(F32), axis=0)


def shard_kernel(gate_ref, up_ref, down_ref, out_ref):
    units, lanes = down_ref.shape[1:]
    out_ref[:, :units] = gate_ref[0]
    out_ref[:, units : 2 * units] = up_ref[0]
    for at in range(0, units, lanes):
        out_ref[:, 2 * units + at : 2 * units + at + lanes] = down_ref[0, at : at + lanes]


def pack_shard(w_gate, w_up, w_down):
    part, units = w_gate.shape[1:]
    return pl.pallas_call(
        shard_kernel,
        in_specs=[pl.BlockSpec(memory_space=pltpu.VMEM)] * 3,
        out_specs=pl.BlockSpec(memory_space=pltpu.VMEM),
        out_shape=jax.ShapeDtypeStruct((part, 3 * units), BF),
    )(w_gate, w_up, w_down)


def on_device(tokens, cotangent, routes, combine, w_gate, w_up, w_down):
    width = tokens.shape[1]
    topk = routes.shape[1]
    shard = pack_shard(w_gate, w_up, w_down)
    weights = lax.all_gather(shard, ("dp", "y"), axis=0)
    weights = weights.reshape((lax.axis_size("dp"), lax.axis_size("y")) + shard.shape)
    mine, other = gather_group(pack(tokens, cotangent, routes, combine))
    cores = lax.axis_size("core")
    first = lax.axis_index("x") * lax.axis_size("y") * cores + lax.axis_index("core")
    first = jnp.stack([first, jnp.full_like(first, cores), lax.axis_index("x")])
    rows, pick, table = route(first, mine, other, weights.shape[1], topk)
    total = sum_group(*experts(first, table, rows, pick, weights, topk))
    tail = total[:, 2 * width :]
    return (
        total[:, :width].astype(BF),
        total[:, width : 2 * width].astype(BF),
        tail[:, :topk] + tail[:, topk : 2 * topk],
    )


def solution(mesh):
    split = Mesh(mesh.devices.reshape(8, 4, 8, 2), ("dp", "x", "y", "core"))
    owner = ("x", "y", "core")
    token = P(("dp",) + owner, None)
    return jax.shard_map(
        on_device,
        mesh=split,
        in_specs=(token,) * 4 + (P(owner, "dp", None), P(owner, "dp", None), P(owner, None, "dp")),
        out_specs=(token, token, token),
        check_vma=False,
    )
```

```python
import functools

import jax
import jax.numpy as jnp
from jax import lax
from jax.experimental import pallas as pl
from jax.experimental.pallas import tpu as pltpu
from jax.sharding import Mesh, PartitionSpec as P

SIZE = 128
SLOTS = 16
CHUNKS = 14
META = 128
BF, F32 = jnp.bfloat16, jnp.float32


def nn(a, b):
    return jnp.dot(a, b, preferred_element_type=F32)


def nt(a, b):
    return lax.dot_general(a, b, (((1,), (1,)), ((), ())), preferred_element_type=F32)


def tn(a, b):
    return lax.dot_general(a, b, (((0,), (0,)), ((), ())), preferred_element_type=F32)


def pack(tokens, cotangent, routes, combine):
    high = combine.astype(BF)
    low = (combine - high.astype(F32)).astype(BF)
    pad = jnp.zeros((tokens.shape[0], META - 3 * routes.shape[1]), BF)
    return jnp.concatenate([tokens, cotangent, routes.astype(BF), high, low, pad], axis=1)


def route_kernel(topk, first_ref, own_ref, other_ref, rows_ref, pick_ref, table_ref, rank_ref):
    local = rank_ref.shape[1]
    blocks, slots, size = pick_ref.shape
    wide = own_ref.shape[1]
    half = blocks // 2
    before = lax.broadcasted_iota(jnp.int32, (size, size), 0) < lax.broadcasted_iota(
        jnp.int32, (size, size), 1
    )
    before = jnp.where(before, 1.0, 0.0).astype(BF)

    def block(b):
        ref = own_ref if b < half else other_ref
        return ref[(b % half) * size : (b % half + 1) * size]

    for b in range(blocks):
        routes = block(b)[:, wide - META :].astype(F32).T[:topk]
        masks = []
        for j in range(local):
            name = (first_ref[0] + j * first_ref[1]).astype(F32)
            masks.append(jnp.max(jnp.where(routes == name, 1.0, 0.0), axis=0, keepdims=True))
        mask = jnp.concatenate(masks, axis=0)
        rank_ref[b] = jnp.where(mask > 0, nn(mask.astype(BF), before), -1.0)
    bases = [jnp.int32(0)]
    for j in range(local):
        count = jnp.max(rank_ref[:, j]).astype(jnp.int32) + 1
        bases.append(bases[j] + (count + SLOTS - 1) // SLOTS)
    chunks = table_ref.shape[0] - 1
    for q in range(chunks):
        at = jnp.int32(0)
        for j in range(local - 1):
            at += (bases[j + 1] <= q).astype(jnp.int32)
        table_ref[q] = at
    table_ref[chunks] = bases[local]
    slot = lax.broadcasted_iota(jnp.int32, (slots, size), 0)
    for b in range(blocks):
        pick = jnp.zeros((slots, size), F32)
        for j in range(local):
            rank = rank_ref[b, j : j + 1]
            where = rank + (bases[j] * SLOTS).astype(F32)
            pick = jnp.where((where == slot.astype(F32)) & (rank >= 0), 1.0, pick)
        pick = pick.astype(BF)
        pick_ref[b] = pick
        rows_ref[:, b] = nn(pick, block(b)).astype(BF).reshape(chunks, SLOTS, wide)


def experts_kernel(topk, first_ref, table_ref, rows_ref, pick_ref, w_ref, own_ref, other_ref, back_ref):
    q = pl.program_id(0)
    chunks = pl.num_programs(0)
    blocks, slots, size = pick_ref.shape
    wide = rows_ref.shape[3]
    width = (wide - META) // 2
    count = blocks * SLOTS
    zs, part = w_ref.shape[0], w_ref.shape[2]
    hidden_units = w_ref.shape[3] // 3

    @pl.when(q >= table_ref[chunks])
    def _():
        back_ref[q] = jnp.zeros(back_ref.shape[1:], BF)

    @pl.when(q < table_ref[chunks])
    def _():
        name = (first_ref[0] + table_ref[q] * first_ref[1]).astype(F32)

        gate_up = w_ref[:, 0, :, : 2 * hidden_units].reshape(zs * part, 2 * hidden_units)
        down = jnp.concatenate(
            [
                jnp.concatenate([w_ref[z, 0, :, at : at + META] for z in range(zs)], axis=1)
                for at in range(2 * hidden_units, 3 * hidden_units, META)
            ],
            axis=0,
        )
        x = rows_ref[0, :, :, :width].reshape(count, width)
        dy = rows_ref[0, :, :, width : 2 * width].reshape(count, width)
        meta = rows_ref[0, :, :, 2 * width :].astype(F32).reshape(count, META)
        lane = lax.broadcasted_iota(jnp.int32, meta.shape, 1)
        hit = (meta == name) & (lane < topk)
        both = pltpu.roll(meta, META - topk, 1) + pltpu.roll(meta, META - 2 * topk, 1)
        g = jnp.sum(jnp.where(hit, both, 0.0), axis=1, keepdims=True)
        pre = nn(x, gate_up)
        gate, up = pre[:, :hidden_units], pre[:, hidden_units:]
        sig = jax.nn.sigmoid(gate)
        silu = gate * sig
        hidden = (silu * up).astype(BF)
        hidden_grad = g * nt(dy, down)
        gate_grad = (hidden_grad * up * sig * (1.0 + gate * (1.0 - sig))).astype(BF)
        up_grad = (hidden_grad * silu).astype(BF)
        eo = nn(hidden, down).astype(BF).astype(F32)
        grad = (nt(jnp.concatenate([gate_grad, up_grad], axis=1), gate_up)).astype(BF)
        cg = jnp.sum(eo * dy.astype(F32), axis=1, keepdims=True)
        cg_high = cg.astype(BF).astype(F32)
        tail = jnp.where(hit, cg_high, 0.0) + pltpu.roll(jnp.where(hit, cg - cg_high, 0.0), topk, 1)
        cut = (blocks, SLOTS)
        back_ref[q, :, :, :width] = (g * eo).astype(BF).reshape(cut + (width,))
        back_ref[q, :, :, width : 2 * width] = grad.reshape(cut + (width,))
        back_ref[q, :, :, 2 * width :] = tail.astype(BF).reshape(cut + (META,))

    @pl.when(q == chunks - 1)
    def _():
        half = blocks // 2
        for b in range(blocks):
            ref = own_ref if b < half else other_ref
            at = lax.rem(first_ref[2] + b % half, half) * size
            ref[pl.ds(pl.multiple_of(at, size), size)] = tn(pick_ref[b], back_ref[:, b].reshape(slots, wide)).astype(BF)


def route(first, own, other, local, topk):
    half, wide = own.shape
    blocks = 2 * half // SIZE
    vmem = pl.BlockSpec(memory_space=pltpu.VMEM)
    smem = pl.BlockSpec(memory_space=pltpu.SMEM)
    return pl.pallas_call(
        functools.partial(route_kernel, topk),
        in_specs=[smem, vmem, vmem],
        out_specs=[vmem, vmem, smem],
        out_shape=[
            jax.ShapeDtypeStruct((CHUNKS, blocks, SLOTS, wide), BF),
            jax.ShapeDtypeStruct((blocks, CHUNKS * SLOTS, SIZE), BF),
            jax.ShapeDtypeStruct((CHUNKS + 1,), jnp.int32),
        ],
        scratch_shapes=[pltpu.VMEM((blocks, local, SIZE), F32)],
        compiler_params=pltpu.CompilerParams(vmem_limit_bytes=24 * 1024 * 1024),
        cost_estimate=pl.CostEstimate(
            flops=2 * 2 * half * CHUNKS * SLOTS * wide, bytes_accessed=18_000_000, transcendentals=0
        ),
    )(first, own, other)


def experts(first, table, rows, pick, weights, topk):
    zs, local, part, hidden = weights.shape
    chunks, blocks, slots, wide = rows.shape
    half = blocks * SIZE // 2
    whole = pl.BlockSpec((half, wide), lambda q, s, t: (0, 0))
    return pl.pallas_call(
        functools.partial(experts_kernel, topk),
        grid_spec=pltpu.PrefetchScalarGridSpec(
            num_scalar_prefetch=2,
            grid=(chunks,),
            in_specs=[
                pl.BlockSpec((1, blocks, slots, wide), lambda q, s, t: (jnp.minimum(q, t[chunks] - 1), 0, 0, 0)),
                pl.BlockSpec(pick.shape, lambda q, s, t: (0, 0, 0)),
                pl.BlockSpec((zs, 1, part, hidden), lambda q, s, t: (0, t[q], 0, 0)),
            ],
            out_specs=[whole, whole],
            scratch_shapes=[pltpu.VMEM(rows.shape, BF)],
        ),
        out_shape=[jax.ShapeDtypeStruct((half, wide), BF)] * 2,
        compiler_params=pltpu.CompilerParams(vmem_limit_bytes=30 * 1024 * 1024),
        cost_estimate=pl.CostEstimate(
            flops=2 * 2 * CHUNKS * SIZE * 1024 * hidden, bytes_accessed=36_000_000, transcendentals=0
        ),
    )(first, table, rows, pick, weights)


def shift(array, axis, by):
    size = lax.axis_size(axis)
    return lax.ppermute(array, axis, [(i, (i + by) % size) for i in range(size)])


def gather_group(own):
    middle = own.shape[0] // 2
    left, right = shift(own, "x", 1), shift(own, "x", -1)
    far = [shift(left[:middle], "x", 1), shift(right[middle:], "x", -1)]
    mine = jnp.concatenate([own, right] + far + [left], axis=0)
    return mine, shift(mine, "core", 1)


def add(a, b):
    return (a.astype(F32) + b.astype(F32)).astype(BF)


def sum_group(mine, other):
    size = lax.axis_size("x")
    total = add(mine, shift(other, "core", 1)).reshape((size, mine.shape[0] // size, mine.shape[1]))
    parts = lax.all_to_all(total, "x", 0, 0, tiled=True)
    return jnp.sum(parts.astype(F32), axis=0)


def shard_kernel(gate_ref, up_ref, down_ref, out_ref):
    units, lanes = down_ref.shape[1:]
    out_ref[:, :units] = gate_ref[0]
    out_ref[:, units : 2 * units] = up_ref[0]
    for at in range(0, units, lanes):
        out_ref[:, 2 * units + at : 2 * units + at + lanes] = down_ref[0, at : at + lanes]


def pack_shard(w_gate, w_up, w_down):
    part, units = w_gate.shape[1:]
    return pl.pallas_call(
        shard_kernel,
        in_specs=[pl.BlockSpec(memory_space=pltpu.VMEM)] * 3,
        out_specs=pl.BlockSpec(memory_space=pltpu.VMEM),
        out_shape=jax.ShapeDtypeStruct((part, 3 * units), BF),
    )(w_gate, w_up, w_down)


def on_device(tokens, cotangent, routes, combine, w_gate, w_up, w_down):
    width = tokens.shape[1]
    topk = routes.shape[1]
    shard = pack_shard(w_gate, w_up, w_down)
    weights = lax.all_gather(shard, ("dp", "y"), axis=0)
    weights = weights.reshape((lax.axis_size("dp"), lax.axis_size("y")) + shard.shape)
    mine, other = gather_group(pack(tokens, cotangent, routes, combine))
    cores = lax.axis_size("core")
    first = lax.axis_index("x") * lax.axis_size("y") * cores + lax.axis_index("core")
    first = jnp.stack([first, jnp.full_like(first, cores), lax.axis_index("x")])
    rows, pick, table = route(first, mine, other, weights.shape[1], topk)
    total = sum_group(*experts(first, table, rows, pick, weights, topk))
    tail = total[:, 2 * width :]
    return (
        total[:, :width].astype(BF),
        total[:, width : 2 * width].astype(BF),
        tail[:, :topk] + tail[:, topk : 2 * topk],
    )


def solution(mesh):
    split = Mesh(mesh.devices.reshape(8, 4, 8, 2), ("dp", "x", "y", "core"))
    owner = ("x", "y", "core")
    token = P(("dp",) + owner, None)
    return jax.shard_map(
        on_device,
        mesh=split,
        in_specs=(token,) * 4 + (P(owner, "dp", None), P(owner, "dp", None), P(owner, None, "dp")),
        out_specs=(token, token, token),
        check_vma=False,
    )
```
